32 devices in a mesh: groups: 2 (over y), blk: 4 (over z), uly: 4 (over x, core).
Axes of the slice: x: 2, y: 2, z: 4, core: 2. Of those that a mesh axis runs over, the one named last changes fastest.
Arguments:
- queries: bfloat16 [2048, 32, 128], P(('groups', 'blk', 'uly')), parts along dimension 0, may hold values from -160 to 160
- key_states: bfloat16 [2048, 32, 128], P(('groups', 'blk', 'uly')), parts along dimension 0, may hold values from -4 to 4
- value_states: bfloat16 [2048, 32, 128], P(('groups', 'blk', 'uly')), parts along dimension 0, may hold values from -6 to 6
- block_list: int32 [16, 8], P('groups'), parts along dimension 0, may hold values from -1 to 7, as said below
- valid_count: int32 [2], P('groups'), parts along dimension 0, may hold values from 897 to 1024
Outputs:
- attended: bfloat16 [2048, 32, 128], P(('groups', 'blk', 'uly')), parts along dimension 0
The draws below stay inside these ranges and needn't reach their ends.
There are 2 independent parts, one for each index of `groups`. The reference program is written for one: setup_inputs(seed, part) draws one part's arguments, and reference() takes and returns one part's arrays. A program takes and returns all parts, laid end to end along the dimension named above; each array names one. Nothing has to cross between parts.
Inputs may be any that keep to these rules, and one draw needn't show every extreme that they name: `block_list`: row i lists, in ascending order, the key blocks that query block i may attend, each once, and the rest of the row is -1; block 0 and block i are always listed.
All inputs are finite; a program needn't handle non-finite values.
Results may differ from the reference program's by a relative error of at most 0.0055.
Values may be sent and summed in bfloat16 or wider, within the bound.
A program may use at most 64 MiB of HBM per device.

```python
import math
import jax
import jax.numpy as jnp
from jax import lax

BLOCK = 128
HD = 128
FRAME_BLK = 28
NBLK = 8
SEQ = 1024
HEADS = 32


def draw_queries(key, part):
    key = jax.random.fold_in(key, 11)
    shape = (SEQ, HEADS, HD)
    query_part = jnp.clip(jax.random.normal(key, shape, jnp.float32), -4.0, 4.0) * 1.5
    return query_part.astype(jnp.bfloat16)


def draw_key_states(key, part):
    key = jax.random.fold_in(key, 12)
    shape = (SEQ, HEADS, HD)
    key_part = jnp.clip(jax.random.normal(key, shape, jnp.float32), -4.0, 4.0)
    return key_part.astype(jnp.bfloat16)


def draw_block_list(key, part):
    key = jax.random.fold_in(key, 5)
    first, second = jax.random.split(key)
    places = jnp.arange(NBLK, dtype=jnp.int32)
    frame = places // FRAME_BLK
    within = places % FRAME_BLK
    breadth = jax.random.randint(first, (), FRAME_BLK // 2, FRAME_BLK + 1)
    jitter = jax.random.randint(second, (NBLK,), 0, 2)
    apart = jnp.abs(frame[:, None] - frame[None, :]) + 1
    level = jnp.zeros((NBLK, NBLK), jnp.int32)
    for power in range(1, 16):
        level = level + (apart >= 2 ** power).astype(jnp.int32)
    reach = jnp.right_shift(breadth, level) + jitter[:, None]
    allowed = (jnp.abs(within[:, None] - within[None, :]) <= reach) | (places[None, :] == 0) | (places[:, None] == places[None, :])
    scores = jnp.where(allowed, places[None, :], NBLK + places[None, :])
    ordered = jnp.sort(scores, axis=1)
    return jnp.where(ordered < NBLK, ordered, -1).astype(jnp.int32)


def block_scale(rng, extent, cuts, low, top_value):
    level = 1.0
    for dim, shards_of in cuts:
        steps = jax.random.uniform(jax.random.fold_in(jax.random.fold_in(rng, 6), dim), (shards_of,), jnp.float32, low / len(cuts), top_value / len(cuts))
        level = level * jnp.repeat(jnp.exp(steps), extent[dim] // shards_of).reshape((-1,) + (1,) * (len(extent) - 1 - dim))
    return level


def scatter_about(own_key, extent, deviation, most, cuts=(), kind=jnp.bfloat16):
    factor_of = block_scale(own_key, extent, cuts, -0.22, 0.18) if cuts else 1.0
    values = jax.random.normal(own_key, extent, jnp.float32) * deviation * factor_of
    return jnp.minimum(jnp.maximum(values, -most), most).astype(kind)


def setup_inputs(seed: int = 0, part: int = 0) -> dict:
    streams_of = jax.random.split(jax.random.key(seed), 6)
    part_splits = jax.random.split(jax.random.fold_in(streams_of[5], part), 6)
    queries = draw_queries(jax.random.fold_in(jax.random.fold_in(streams_of[5], part), 71), part)
    key_states = draw_key_states(jax.random.fold_in(jax.random.fold_in(streams_of[5], part), 71), part)
    value_states = scatter_about(part_splits[2], (SEQ, HEADS, HD), 1.0, 6.0, ((0, 16),))
    block_list = draw_block_list(jax.random.fold_in(jax.random.fold_in(streams_of[5], part), 71), part)
    valid_count = jax.random.randint(part_splits[4], (1,), SEQ - BLOCK + 1, SEQ + 1).astype(jnp.int32)
    return {"queries": queries, "key_states": key_states, "value_states": value_states, "block_list": block_list, "valid_count": valid_count}


def reference(queries, key_states, value_states, block_list, valid_count):
    block_total = block_list.shape[0]
    allowed = jnp.any(block_list[:, :, None] == jnp.arange(block_total, dtype=jnp.int32)[None, None, :], axis=1)
    key_places = jnp.arange(SEQ, dtype=jnp.int32)
    key_live = key_places < valid_count[0]
    keys_wide = key_states.astype(jnp.float32)
    values_wide = value_states.astype(jnp.float32)
    factor = 1.0 / math.sqrt(HD)

    def one_block(index):
        start = index * BLOCK
        query_rows = lax.dynamic_slice_in_dim(queries, start, BLOCK, 0).astype(jnp.float32)
        scores = jnp.einsum('qhd,khd->hqk', query_rows, keys_wide) * factor
        live = jnp.repeat(allowed[index], BLOCK, total_repeat_length=SEQ) & key_live
        masked = jnp.where(live[None, None, :], scores, -1e+30)
        highest = lax.optimization_barrier(jnp.max(masked, axis=-1, keepdims=True))
        weights = jnp.where(live[None, None, :], jnp.exp(masked - highest), 0.0)
        totals = lax.optimization_barrier(jnp.sum(weights, axis=-1))
        rounded = lax.optimization_barrier(weights.astype(jnp.bfloat16)).astype(jnp.float32)
        mixed = jnp.einsum('hqk,khd->qhd', rounded, values_wide)
        mixed = mixed / jnp.transpose(totals)[:, :, None]
        return mixed.astype(jnp.bfloat16)
    pieces = lax.map(one_block, jnp.arange(block_total, dtype=jnp.int32))
    return pieces.reshape(SEQ, HEADS, HD)
```

```python
import functools
import math

import jax
import jax.numpy as jnp
from jax import lax
from jax.experimental import pallas as pl
from jax.experimental.pallas import tpu as pltpu
from jax.sharding import PartitionSpec as P

BLOCK = 128


def from_behind(value, axis, steps):
    count = lax.axis_size(axis)
    pairs = [(source, (source + steps) % count) for source in range(count)]
    return lax.ppermute(value, axis, pairs)


def local(queries, key_states, value_states, block_list, valid_count):
    blk_count = lax.axis_size("blk")
    uly_count = lax.axis_size("uly")
    my_place = lax.axis_index("blk")
    entry_rows = queries.shape[0]
    head_count = queries.shape[1]
    head_size = queries.shape[2]
    local_heads = head_count // uly_count
    row_count = entry_rows * uly_count
    own_queries, own_keys, own_values = (
        lax.all_to_all(queries, "uly", split_axis=1, concat_axis=0, tiled=True),
        lax.all_to_all(key_states, "uly", split_axis=1, concat_axis=0, tiled=True),
        lax.all_to_all(value_states, "uly", split_axis=1, concat_axis=0, tiled=True),
    )

    def token_places(owner):
        return owner * row_count + jnp.arange(row_count, dtype=jnp.int32)

    block_total = block_list.shape[0]
    allowed = jnp.any(
        block_list[:, :, None] == jnp.arange(block_total, dtype=jnp.int32)[None, None, :], axis=1
    )
    query_mask = jnp.take(allowed, token_places(my_place) // BLOCK, axis=0)
    limit = valid_count[0]
    factor = 1.0 / math.sqrt(head_size)

    def accumulate(state, key_value, live):
        highest, totals, summed = state
        scores = (
            jnp.einsum(
                "qhd,khd->hqk", own_queries, key_value[0], preferred_element_type=jnp.float32
            )
            * factor
        )
        masked = jnp.where(live[None], scores, -1e30)
        new_high = jnp.maximum(highest, jnp.max(masked, axis=-1))
        rescale = jnp.exp(highest - new_high)
        weights = jnp.where(live[None], jnp.exp(masked - new_high[:, :, None]), 0.0)
        totals = totals * rescale + jnp.sum(weights, axis=-1)
        summed = summed * rescale[:, :, None] + jnp.einsum(
            "hqk,khd->hqd",
            weights.astype(jnp.bfloat16),
            key_value[1],
            preferred_element_type=jnp.float32,
        )
        return (new_high, totals, summed)

    def attend(state, key_value, owner):
        key_spots = token_places(owner)
        live = jnp.take(query_mask, key_spots // BLOCK, axis=1) & (key_spots < limit)[None, :]
        return accumulate(state, key_value, live)

    start_state = (
        jnp.full((local_heads, row_count), -1e30, jnp.float32),
        jnp.zeros((local_heads, row_count), jnp.float32),
        jnp.zeros((local_heads, row_count, head_size), jnp.float32),
    )
    held = jnp.stack([own_keys, own_values])
    state = attend(start_state, held, my_place)

    def visit(hop_index, carried):
        travelling, inner = carried
        travelling = from_behind(travelling, "blk", 1)
        owner = (my_place - hop_index) % blk_count
        return (travelling, attend(inner, travelling, owner))

    _, (highest, totals, summed) = lax.fori_loop(1, blk_count, visit, (held, state))
    result = (summed / totals[:, :, None]).astype(jnp.bfloat16)
    result = jnp.transpose(result, (1, 0, 2))
    return lax.all_to_all(result, "uly", split_axis=0, concat_axis=1, tiled=True)


MESH = pl.DeviceIdType.MESH
DEAD = -1e30


def exchange_kernel(
    chips,
    uly_count,
    heads,
    rows,
    q_in,
    k_in,
    v_in,
    list_ref,
    count_ref,
    out_ref,
    q_buf,
    k_buf,
    v_buf,
    o_buf,
    bias_ref,
    in_send,
    in_recv,
    out_send,
    out_recv,
    own_sem,
    own_out_sem,
):
    me = lax.axis_index("blk") * uly_count + lax.axis_index("uly")
    my_chip = me // 2
    my_core = me % 2
    sibling = my_chip * 2 + 1 - my_core
    sources = (k_in, v_in, q_in)
    buffers = (k_buf, v_buf, q_buf)
    seq = chips * 2 * rows

    def place(device):
        return {"blk": device // uly_count, "uly": device % uly_count}

    def partner(step):
        chip = 0
        bit = 1
        while bit < chips:
            chip = chip + ((my_chip // bit + step // bit) % 2) * bit
            bit *= 2
        return chip

    def token_rows(device):
        return pl.ds(pl.multiple_of(device * rows, rows), rows)

    def in_copy(kind, head, step, device, dest_core):
        return pltpu.make_async_remote_copy(
            src_ref=sources[kind].at[device * heads + head],
            dst_ref=buffers[kind].at[head, token_rows(me)],
            send_sem=in_send.at[kind, head, step, dest_core],
            recv_sem=in_recv.at[kind, head, step, my_core],
            device_id=place(device),
            device_id_type=MESH,
        )

    def in_wait(kind, head, step, device, source_core):
        pltpu.make_async_remote_copy(
            src_ref=sources[kind].at[device * heads + head],
            dst_ref=buffers[kind].at[head, token_rows(device)],
            send_sem=in_send.at[kind, head, step, source_core],
            recv_sem=in_recv.at[kind, head, step, source_core],
            device_id=place(device),
            device_id_type=MESH,
        ).wait_recv()

    def own_copy(kind, head):
        return pltpu.make_async_copy(
            sources[kind].at[me * heads + head],
            buffers[kind].at[head, token_rows(me)],
            own_sem.at[kind, head],
        )

    def out_copy(head, step, device, dest_core):
        return pltpu.make_async_remote_copy(
            src_ref=o_buf.at[head, token_rows(device)],
            dst_ref=out_ref.at[me * heads + head],
            send_sem=out_send.at[head, step, dest_core],
            recv_sem=out_recv.at[head, step, my_core],
            device_id=place(device),
            device_id_type=MESH,
        )

    def out_wait(head, step, device, source_core):
        pltpu.make_async_remote_copy(
            src_ref=o_buf.at[head, token_rows(device)],
            dst_ref=out_ref.at[device * heads + head],
            send_sem=out_send.at[head, step, source_core],
            recv_sem=out_recv.at[head, step, source_core],
            device_id=place(device),
            device_id_type=MESH,
        ).wait_recv()

    def own_out(head):
        return pltpu.make_async_copy(
            o_buf.at[head, token_rows(me)], out_ref.at[me * heads + head], own_out_sem.at[head]
        )

    def each_partner(body):
        def visit(index, carried):
            step = chips - 1 - index
            chip = partner(step)
            for core in range(2):
                body(step, chip * 2 + core, core)
            return carried

        lax.fori_loop(0, chips - 1, visit, 0)

    barrier = pltpu.get_barrier_semaphore()

    def greet(step, device, core):
        pl.semaphore_signal(barrier, inc=1, device_id=place(device), device_id_type=MESH)

    each_partner(greet)
    pl.semaphore_signal(barrier, inc=1, device_id=place(sibling), device_id_type=MESH)
    for head in range(heads):
        for kind in range(3):
            own_copy(kind, head).start()
    pl.semaphore_wait(barrier, chips * 2 - 1)

    for head in range(heads):
        for kind in range(3):
            each_partner(
                lambda step, device, core: in_copy(kind, head, step, device, core).start()
            )
            in_copy(kind, head, 0, sibling, 0).start()

    block_total = list_ref.shape[0]
    spots = lax.broadcasted_iota(jnp.int32, (block_total, seq), 1)
    owners = spots // BLOCK
    listed = list_ref[...]
    live = owners == listed[:, 0:1]
    for column in range(1, block_total):
        live = live | (owners == listed[:, column : column + 1])
    live = live & (spots < count_ref[0])
    bias_ref[...] = jnp.where(live, 0.0, DEAD)
    factor = (1.0 / math.sqrt(q_buf.shape[2])) * math.log2(math.e)
    chip_rows = 2 * rows

    def attend(head, chip):
        span = pl.ds(pl.multiple_of(chip * chip_rows, chip_rows), chip_rows)
        scores = lax.dot_general(
            q_buf[head, span, :],
            k_buf[head],
            (((1,), (1,)), ((), ())),
            preferred_element_type=jnp.float32,
        )
        bias = bias_ref[pl.ds(chip * chip_rows // BLOCK, 1), :]
        masked = scores * factor + bias
        highest = jnp.max(masked, axis=-1, keepdims=True)
        weights = jnp.exp2(masked - highest)
        totals = jnp.sum(weights, axis=-1, keepdims=True)
        mixed = jnp.dot(
            weights.astype(jnp.bfloat16), v_buf[head], preferred_element_type=jnp.float32
        )
        o_buf[head, span, :] = (mixed / totals).astype(jnp.bfloat16)

    def wait_sibling(kind, head):
        pltpu.make_async_remote_copy(
            src_ref=sources[kind].at[sibling * heads + head],
            dst_ref=buffers[kind].at[head, token_rows(sibling)],
            send_sem=in_send.at[kind, head, 0, 0],
            recv_sem=in_recv.at[kind, head, 0, 1 - my_core],
            device_id=place(sibling),
            device_id_type=MESH,
        ).wait_recv()

    for head in range(heads):
        for kind in range(2):
            own_copy(kind, head).wait()
            wait_sibling(kind, head)
            each_partner(
                lambda step, device, core: in_wait(kind, head, step, device, core)
            )

        def work(index, carried):
            step = chips - 1 - index
            chip = partner(step)
            for core in range(2):
                in_wait(2, head, step, chip * 2 + core, core)
            attend(head, chip)
            for core in range(2):
                out_copy(head, step, chip * 2 + core, core).start()
            return carried

        lax.fori_loop(0, chips - 1, work, 0)
        own_copy(2, head).wait()
        wait_sibling(2, head)
        attend(head, my_chip)
        out_copy(head, 0, sibling, 0).start()
        own_out(head).start()

    for head in range(heads):
        for kind in range(3):
            each_partner(
                lambda step, device, core: in_copy(kind, head, step, device, core).wait_send()
            )
            in_copy(kind, head, 0, sibling, 0).wait_send()
        each_partner(
            lambda step, device, core: out_copy(head, step, device, core).wait_send()
        )
        out_copy(head, 0, sibling, 0).wait_send()
        each_partner(lambda step, device, core: out_wait(head, step, device, core))
        pltpu.make_async_remote_copy(
            src_ref=o_buf.at[head, token_rows(sibling)],
            dst_ref=out_ref.at[sibling * heads + head],
            send_sem=out_send.at[head, 0, 0],
            recv_sem=out_recv.at[head, 0, 1 - my_core],
            device_id=place(sibling),
            device_id_type=MESH,
        ).wait_recv()
        own_out(head).wait()


def whole_heads(blk_count, uly_count, queries, key_states, value_states, block_list, valid_count):
    rows, head_count, head_size = queries.shape
    devices = blk_count * uly_count
    chips = devices // 2
    heads = head_count // devices
    seq = rows * devices

    def by_head(value):
        return jnp.transpose(value, (1, 0, 2))

    result = pl.pallas_call(
        functools.partial(exchange_kernel, chips, uly_count, heads, rows),
        out_shape=jax.ShapeDtypeStruct((head_count, rows, head_size), jnp.bfloat16),
        in_specs=[pl.BlockSpec(memory_space=pl.ANY)] * 3
        + [
            pl.BlockSpec(memory_space=pltpu.VMEM),
            pl.BlockSpec(memory_space=pltpu.SMEM),
        ],
        out_specs=pl.BlockSpec(memory_space=pl.ANY),
        scratch_shapes=[pltpu.VMEM((heads, seq, head_size), jnp.bfloat16)] * 4
        + [
            pltpu.VMEM((block_list.shape[0], seq), jnp.float32),
            pltpu.SemaphoreType.DMA((3, heads, chips, 2)),
            pltpu.SemaphoreType.DMA((3, heads, chips, 2)),
            pltpu.SemaphoreType.DMA((heads, chips, 2)),
            pltpu.SemaphoreType.DMA((heads, chips, 2)),
            pltpu.SemaphoreType.DMA((3, heads)),
            pltpu.SemaphoreType.DMA((heads,)),
        ],
        compiler_params=pltpu.CompilerParams(
            collective_id=0, has_side_effects=True, vmem_limit_bytes=32 * 1024 * 1024
        ),
    )(by_head(queries), by_head(key_states), by_head(value_states), block_list, valid_count)
    return jnp.transpose(result, (1, 0, 2))


def fits_whole_heads(blk_count, uly_count, rows, head_count):
    devices = blk_count * uly_count
    return (
        head_count % devices == 0
        and devices >= 4
        and devices & (devices - 1) == 0
        and uly_count % 2 == 0
        and BLOCK % (2 * rows) == 0
        and rows % 16 == 0
    )


def solution(mesh):
    blk_count, uly_count = mesh.shape["blk"], mesh.shape["uly"]

    def step(queries, *rest):
        rows, head_count, _ = queries.shape
        if fits_whole_heads(blk_count, uly_count, rows, head_count):
            return whole_heads(blk_count, uly_count, queries, *rest)
        return local(queries, *rest)

    placed = (
        P(("groups", "blk", "uly"), None, None),
        P(("groups", "blk", "uly"), None, None),
        P(("groups", "blk", "uly"), None, None),
        P("groups", None),
        P("groups"),
    )
    return jax.shard_map(
        step,
        mesh=mesh,
        in_specs=placed,
        out_specs=P(("groups", "blk", "uly"), None, None),
        check_vma=False,
    )
```

```python
import functools
import math

import jax
import jax.numpy as jnp
from jax import lax
from jax.experimental import pallas as pl
from jax.experimental.pallas import tpu as pltpu
from jax.sharding import PartitionSpec as P

BLOCK = 128


def from_behind(value, axis, steps):
    count = lax.axis_size(axis)
    pairs = [(source, (source + steps) % count) for source in range(count)]
    return lax.ppermute(value, axis, pairs)


def local(queries, key_states, value_states, block_list, valid_count):
    blk_count = lax.axis_size("blk")
    uly_count = lax.axis_size("uly")
    my_place = lax.axis_index("blk")
    entry_rows = queries.shape[0]
    head_count = queries.shape[1]
    head_size = queries.shape[2]
    local_heads = head_count // uly_count
    row_count = entry_rows * uly_count
    own_queries, own_keys, own_values = (
        lax.all_to_all(queries, "uly", split_axis=1, concat_axis=0, tiled=True),
        lax.all_to_all(key_states, "uly", split_axis=1, concat_axis=0, tiled=True),
        lax.all_to_all(value_states, "uly", split_axis=1, concat_axis=0, tiled=True),
    )

    def token_places(owner):
        return owner * row_count + jnp.arange(row_count, dtype=jnp.int32)

    block_total = block_list.shape[0]
    allowed = jnp.any(
        block_list[:, :, None] == jnp.arange(block_total, dtype=jnp.int32)[None, None, :], axis=1
    )
    query_mask = jnp.take(allowed, token_places(my_place) // BLOCK, axis=0)
    limit = valid_count[0]
    factor = 1.0 / math.sqrt(head_size)

    def accumulate(state, key_value, live):
        highest, totals, summed = state
        scores = (
            jnp.einsum(
                "qhd,khd->hqk", own_queries, key_value[0], preferred_element_type=jnp.float32
            )
            * factor
        )
        masked = jnp.where(live[None], scores, -1e30)
        new_high = jnp.maximum(highest, jnp.max(masked, axis=-1))
        rescale = jnp.exp(highest - new_high)
        weights = jnp.where(live[None], jnp.exp(masked - new_high[:, :, None]), 0.0)
        totals = totals * rescale + jnp.sum(weights, axis=-1)
        summed = summed * rescale[:, :, None] + jnp.einsum(
            "hqk,khd->hqd",
            weights.astype(jnp.bfloat16),
            key_value[1],
            preferred_element_type=jnp.float32,
        )
        return (new_high, totals, summed)

    def attend(state, key_value, owner):
        key_spots = token_places(owner)
        live = jnp.take(query_mask, key_spots // BLOCK, axis=1) & (key_spots < limit)[None, :]
        return accumulate(state, key_value, live)

    start_state = (
        jnp.full((local_heads, row_count), -1e30, jnp.float32),
        jnp.zeros((local_heads, row_count), jnp.float32),
        jnp.zeros((local_heads, row_count, head_size), jnp.float32),
    )
    held = jnp.stack([own_keys, own_values])
    state = attend(start_state, held, my_place)

    def visit(hop_index, carried):
        travelling, inner = carried
        travelling = from_behind(travelling, "blk", 1)
        owner = (my_place - hop_index) % blk_count
        return (travelling, attend(inner, travelling, owner))

    _, (highest, totals, summed) = lax.fori_loop(1, blk_count, visit, (held, state))
    result = (summed / totals[:, :, None]).astype(jnp.bfloat16)
    result = jnp.transpose(result, (1, 0, 2))
    return lax.all_to_all(result, "uly", split_axis=0, concat_axis=1, tiled=True)


MESH = pl.DeviceIdType.MESH
DEAD = -1e30


def exchange_kernel(
    chips,
    uly_count,
    heads,
    rows,
    q_hbm,
    k_hbm,
    v_hbm,
    list_hbm,
    count_ref,
    out_ref,
    list_ref,
    q_raw,
    k_raw,
    v_raw,
    q_in,
    k_in,
    v_in,
    q_buf,
    k_buf,
    v_buf,
    o_buf,
    bias_ref,
    in_send,
    in_recv,
    out_send,
    out_recv,
    own_sem,
    own_out_sem,
    load_sem,
):
    me = lax.axis_index("blk") * uly_count + lax.axis_index("uly")
    my_chip = me // 2
    my_core = me % 2
    sibling = my_chip * 2 + 1 - my_core
    sources = (k_in, v_in, q_in)
    buffers = (k_buf, v_buf, q_buf)
    seq = chips * 2 * rows

    def place(device):
        return {"blk": device // uly_count, "uly": device % uly_count}

    def partner(step):
        chip = 0
        bit = 1
        while bit < chips:
            chip = chip + ((my_chip // bit + step // bit) % 2) * bit
            bit *= 2
        return chip

    def token_rows(device):
        return pl.ds(pl.multiple_of(device * rows, rows), rows)

    def in_copy(kind, head, step, device, dest_core):
        return pltpu.make_async_remote_copy(
            src_ref=sources[kind].at[device * heads + head],
            dst_ref=buffers[kind].at[head, token_rows(me)],
            send_sem=in_send.at[kind, head, step, dest_core],
            recv_sem=in_recv.at[kind, head, step, my_core],
            device_id=place(device),
            device_id_type=MESH,
        )

    def in_wait(kind, head, step, device, source_core):
        pltpu.make_async_remote_copy(
            src_ref=sources[kind].at[device * heads + head],
            dst_ref=buffers[kind].at[head, token_rows(device)],
            send_sem=in_send.at[kind, head, step, source_core],
            recv_sem=in_recv.at[kind, head, step, source_core],
            device_id=place(device),
            device_id_type=MESH,
        ).wait_recv()

    def own_copy(kind, head):
        return pltpu.make_async_copy(
            sources[kind].at[me * heads + head],
            buffers[kind].at[head, token_rows(me)],
            own_sem.at[kind, head],
        )

    def out_copy(head, step, device, dest_core):
        return pltpu.make_async_remote_copy(
            src_ref=o_buf.at[head, token_rows(device)],
            dst_ref=out_ref.at[me * heads + head],
            send_sem=out_send.at[head, step, dest_core],
            recv_sem=out_recv.at[head, step, my_core],
            device_id=place(device),
            device_id_type=MESH,
        )

    def out_wait(head, step, device, source_core):
        pltpu.make_async_remote_copy(
            src_ref=o_buf.at[head, token_rows(device)],
            dst_ref=out_ref.at[device * heads + head],
            send_sem=out_send.at[head, step, source_core],
            recv_sem=out_recv.at[head, step, source_core],
            device_id=place(device),
            device_id_type=MESH,
        ).wait_recv()

    def own_out(head):
        return pltpu.make_async_copy(
            o_buf.at[head, token_rows(me)], out_ref.at[me * heads + head], own_out_sem.at[head]
        )

    def each_partner(body):
        def visit(index, carried):
            step = 1 + index
            chip = partner(step)
            for core in range(2):
                body(step, chip * 2 + core, core)
            return carried

        lax.fori_loop(0, chips - 1, visit, 0)

    loads = [
        pltpu.make_async_copy(whole, raw, load_sem.at[kind])
        for kind, (whole, raw) in enumerate(
            ((k_hbm, k_raw), (v_hbm, v_raw), (q_hbm, q_raw), (list_hbm, list_ref))
        )
    ]
    for load in loads:
        load.start()

    def by_head(kind):
        loads[kind].wait()
        raw = (k_raw, v_raw, q_raw)[kind]
        for start in range(0, rows, 16):
            sources[kind][:, start : start + 16, :] = jnp.transpose(
                raw[start : start + 16], (1, 0, 2)
            )

    barrier = pltpu.get_barrier_semaphore()

    def greet(step, device, core):
        pl.semaphore_signal(barrier, inc=1, device_id=place(device), device_id_type=MESH)

    each_partner(greet)
    pl.semaphore_signal(barrier, inc=1, device_id=place(sibling), device_id_type=MESH)
    by_head(0)
    pl.semaphore_wait(barrier, chips * 2 - 1)
    for head in range(heads):
        for kind in range(3):
            if head == 0 and kind > 0:
                by_head(kind)
            own_copy(kind, head).start()
            each_partner(
                lambda step, device, core: in_copy(kind, head, step, device, core).start()
            )
            in_copy(kind, head, 0, sibling, 0).start()

    loads[3].wait()
    block_total = list_ref.shape[0]
    spots = lax.broadcasted_iota(jnp.int32, (block_total, seq), 1)
    owners = spots // BLOCK
    listed = list_ref[...]
    live = owners == listed[:, 0:1]
    for column in range(1, block_total):
        live = live | (owners == listed[:, column : column + 1])
    live = live & (spots < count_ref[0])
    bias_ref[...] = jnp.where(live, 0.0, DEAD)
    factor = (1.0 / math.sqrt(q_buf.shape[2])) * math.log2(math.e)
    chip_rows = 2 * rows

    def attend(head, chip):
        span = pl.ds(pl.multiple_of(chip * chip_rows, chip_rows), chip_rows)
        scores = lax.dot_general(
            q_buf[head, span, :],
            k_buf[head],
            (((1,), (1,)), ((), ())),
            preferred_element_type=jnp.float32,
        )
        bias = bias_ref[pl.ds(chip * chip_rows // BLOCK, 1), :]
        masked = scores * factor + bias
        highest = jnp.max(masked, axis=-1, keepdims=True)
        weights = jnp.exp2(masked - highest)
        totals = jnp.sum(weights, axis=-1, keepdims=True)
        mixed = jnp.dot(
            weights.astype(jnp.bfloat16), v_buf[head], preferred_element_type=jnp.float32
        )
        o_buf[head, span, :] = (mixed / totals).astype(jnp.bfloat16)

    def wait_sibling(kind, head):
        pltpu.make_async_remote_copy(
            src_ref=sources[kind].at[sibling * heads + head],
            dst_ref=buffers[kind].at[head, token_rows(sibling)],
            send_sem=in_send.at[kind, head, 0, 0],
            recv_sem=in_recv.at[kind, head, 0, 1 - my_core],
            device_id=place(sibling),
            device_id_type=MESH,
        ).wait_recv()

    for head in range(heads):
        for kind in range(2):
            own_copy(kind, head).wait()
            wait_sibling(kind, head)
            each_partner(
                lambda step, device, core: in_wait(kind, head, step, device, core)
            )

        def work(index, carried):
            step = 1 + index
            chip = partner(step)
            for core in range(2):
                in_wait(2, head, step, chip * 2 + core, core)
            attend(head, chip)
            for core in range(2):
                out_copy(head, step, chip * 2 + core, core).start()
            return carried

        lax.fori_loop(0, chips - 1, work, 0)
        own_copy(2, head).wait()
        wait_sibling(2, head)
        attend(head, my_chip)
        out_copy(head, 0, sibling, 0).start()
        own_out(head).start()

    for head in range(heads):
        for kind in range(3):
            each_partner(
                lambda step, device, core: in_copy(kind, head, step, device, core).wait_send()
            )
            in_copy(kind, head, 0, sibling, 0).wait_send()
        each_partner(
            lambda step, device, core: out_copy(head, step, device, core).wait_send()
        )
        out_copy(head, 0, sibling, 0).wait_send()
        each_partner(lambda step, device, core: out_wait(head, step, device, core))
        pltpu.make_async_remote_copy(
            src_ref=o_buf.at[head, token_rows(sibling)],
            dst_ref=out_ref.at[sibling * heads + head],
            send_sem=out_send.at[head, 0, 0],
            recv_sem=out_recv.at[head, 0, 1 - my_core],
            device_id=place(sibling),
            device_id_type=MESH,
        ).wait_recv()
        own_out(head).wait()


def whole_heads(blk_count, uly_count, queries, key_states, value_states, block_list, valid_count):
    rows, head_count, head_size = queries.shape
    devices = blk_count * uly_count
    chips = devices // 2
    heads = head_count // devices
    seq = rows * devices

    result = pl.pallas_call(
        functools.partial(exchange_kernel, chips, uly_count, heads, rows),
        out_shape=jax.ShapeDtypeStruct((head_count, rows, head_size), jnp.bfloat16),
        in_specs=[pl.BlockSpec(memory_space=pltpu.HBM)] * 3
        + [
            pl.BlockSpec(memory_space=pltpu.HBM),
            pl.BlockSpec(memory_space=pltpu.SMEM),
        ],
        out_specs=pl.BlockSpec(memory_space=pl.ANY),
        scratch_shapes=[pltpu.VMEM(block_list.shape, jnp.int32)]
        + [pltpu.VMEM((rows, head_count, head_size), jnp.bfloat16)] * 3
        + [pltpu.VMEM((head_count, rows, head_size), jnp.bfloat16)] * 3
        + [pltpu.VMEM((heads, seq, head_size), jnp.bfloat16)] * 4
        + [
            pltpu.VMEM((block_list.shape[0], seq), jnp.float32),
            pltpu.SemaphoreType.DMA((3, heads, chips, 2)),
            pltpu.SemaphoreType.DMA((3, heads, chips, 2)),
            pltpu.SemaphoreType.DMA((heads, chips, 2)),
            pltpu.SemaphoreType.DMA((heads, chips, 2)),
            pltpu.SemaphoreType.DMA((3, heads)),
            pltpu.SemaphoreType.DMA((heads,)),
            pltpu.SemaphoreType.DMA((4,)),
        ],
        compiler_params=pltpu.CompilerParams(
            collective_id=0, has_side_effects=True, vmem_limit_bytes=54528 * 1024
        ),
    )(queries, key_states, value_states, block_list, valid_count)
    return jnp.transpose(result, (1, 0, 2))


def fits_whole_heads(blk_count, uly_count, rows, head_count):
    devices = blk_count * uly_count
    return (
        head_count % devices == 0
        and devices >= 4
        and devices & (devices - 1) == 0
        and uly_count % 2 == 0
        and BLOCK % (2 * rows) == 0
        and rows % 16 == 0
    )


def solution(mesh):
    blk_count, uly_count = mesh.shape["blk"], mesh.shape["uly"]

    def step(queries, *rest):
        rows, head_count, _ = queries.shape
        if fits_whole_heads(blk_count, uly_count, rows, head_count):
            return whole_heads(blk_count, uly_count, queries, *rest)
        return local(queries, *rest)

    placed = (
        P(("groups", "blk", "uly"), None, None),
        P(("groups", "blk", "uly"), None, None),
        P(("groups", "blk", "uly"), None, None),
        P("groups", None),
        P("groups"),
    )
    return jax.shard_map(
        step,
        mesh=mesh,
        in_specs=placed,
        out_specs=P(("groups", "blk", "uly"), None, None),
        check_vma=False,
    )
```
